256 devices in a mesh: leaf: 64 (over x, z, core), level: 4 (over y).
Axes of the slice: x: 4, y: 4, z: 8, core: 2. Of those that a mesh axis runs over, the one named last changes fastest.
Arguments:
- unknowns: bfloat16 [1024, 256, 1024], P(('leaf', 'level')), may hold values from -6 to 6
- leaf_basis: bfloat16 [1024, 256, 64], P(('leaf', 'level')), may hold values from -0.375 to 0.375
- leaf_transfer: bfloat16 [1024, 64, 64], P(('leaf', 'level')), may hold values from -0.75 to 0.75
- parent_transfer: bfloat16 [256, 64, 64], P(('leaf', 'level')), may hold values from -0.75 to 0.75
- near_blocks: bfloat16 [1024, 8, 256, 256], P(('leaf', 'level')), may hold values from -0.125 to 0.125
- near_offset: int32 [1024, 8], P(('leaf', 'level')), may hold values from -4 to 4, as said below
- leaf_blocks: bfloat16 [1024, 6, 64, 64], P(('leaf', 'level')), may hold values from -0.3125 to 0.3125
- leaf_partner: int32 [1024, 6], P(('leaf', 'level')), may hold values from -4 to 4, as said below
- leaf_count: int32 [1024], P(('leaf', 'level')), may hold values from 3 to 6
- top_blocks: bfloat16 [64, 32, 64, 64], P('leaf', 'level'), may hold values from -0.125 to 0.125
- top_source: int32 [64, 32], P('leaf'), may hold values from 0 to 63
- top_count: int32 [64], P('leaf'), may hold values from 8 to 32
Outputs:
- product: float32 [1024, 256, 1024], P(('leaf', 'level'))
The draws below stay inside these ranges and needn't reach their ends.
Inputs may be any that keep to these rules, and one draw needn't show every extreme that they name: `near_offset`: each row holds 8 different offsets, the first of them 0. `leaf_partner`: each row holds 6 different nonzero offsets. `top_source`: sources may repeat within a row.
All inputs are finite; a program needn't handle non-finite values.
Results may differ from the reference program's by a relative error of at most 0.005.
Values may be sent and summed in bfloat16 or wider, within the bound.
No kernel may reach another device: no remote copies, remote signals or barrier semaphores. Data moves between devices by JAX's collectives and lax.ppermute only.
A program may use at most 128 MiB of HBM per device.

```python
import jax
import jax.numpy as jnp
from jax import lax

LEAF = 256
RANK = 64
NRHS = 1024
LEAF_DEV = 4
NEAR = 8
KL = 6
KT = 32
LEAVES = 1024
PARENTS = 256
ROOTS = 64
N_LEVEL = 4


def distinct_offsets(key, count):
    keys = jax.random.split(key, LEAVES)
    chosen = jax.vmap(lambda single_key: jax.random.permutation(single_key, 2 * LEAF_DEV))(keys)[:, :count]
    return jnp.where(chosen < LEAF_DEV, chosen - LEAF_DEV, chosen - LEAF_DEV + 1).astype(jnp.int32)


def draw_near_offset(key, part):
    key = jax.random.fold_in(key, 11)
    others = distinct_offsets(key, NEAR - 1)
    return jnp.concatenate([jnp.zeros((LEAVES, 1), jnp.int32), others], axis=1)


def draw_leaf_partner(key, part):
    key = jax.random.fold_in(key, 12)
    return distinct_offsets(key, KL)


def draw_leaf_count(key, part):
    key = jax.random.fold_in(key, 13)
    counts = jax.random.randint(key, (LEAVES,), KL // 2, KL + 1, dtype=jnp.int32)
    forced = jnp.arange(LEAVES, dtype=jnp.int32) % 5 == 0
    return jnp.where(forced, KL, counts).astype(jnp.int32)


def draw_top_count(key, part):
    key = jax.random.fold_in(key, 14)
    counts = jax.random.randint(key, (ROOTS,), KT // N_LEVEL, KT + 1, dtype=jnp.int32)
    forced = jnp.arange(ROOTS, dtype=jnp.int32) % 5 == 0
    return jnp.where(forced, KT, counts).astype(jnp.int32)


def touch_ends(values, stream_key, low, top_value):
    place = [jax.random.randint(jax.random.fold_in(stream_key, axis), (), 0, length) for axis, length in enumerate(values.shape)]
    main_axis = values.shape.index(max(values.shape))
    beside = place[:main_axis] + [(place[main_axis] + 1) % values.shape[main_axis]] + place[main_axis + 1:]
    return values.at[tuple(place)].set(low).at[tuple(beside)].set(top_value)


def level_of(stream_key, dims, pieces, low, largest):
    def one(axis_at, parts):
        draws = jax.random.uniform(jax.random.fold_in(jax.random.fold_in(stream_key, 6), axis_at), (parts,), jnp.float32, low / len(pieces), largest / len(pieces))
        return jnp.repeat(jnp.exp(draws), dims[axis_at] // parts).reshape((-1,) + (1,) * (len(dims) - axis_at - 1))

    gain = one(*pieces[0])
    for cut in pieces[1:]:
        gain = gain * one(*cut)
    return gain


def bell_draw(own_key, shape, width, most, cuts=(), kind=jnp.bfloat16):
    loudness = level_of(own_key, shape, cuts, -0.22, 0.18) if cuts else 1.0
    drawn = jax.random.normal(own_key, shape, jnp.float32) * width * loudness
    return jnp.minimum(jnp.maximum(drawn, -most), most).astype(kind)


def setup_inputs(seed: int = 0) -> dict:
    arg_keys = jax.random.split(jax.random.key(seed), 13)
    return {
        "unknowns": bell_draw(arg_keys[0], (LEAVES, LEAF, NRHS), 1.0, 6.0, ((0, 256),)),
        "leaf_basis": bell_draw(arg_keys[1], (LEAVES, LEAF, RANK), LEAF ** -0.5, 0.375, ((0, 256),)),
        "leaf_transfer": bell_draw(arg_keys[2], (LEAVES, RANK, RANK), RANK ** -0.5, 0.75, ((0, 256),)),
        "parent_transfer": bell_draw(arg_keys[3], (PARENTS, RANK, RANK), RANK ** -0.5, 0.75, ((0, 256),)),
        "near_blocks": bell_draw(arg_keys[4], (LEAVES, NEAR, LEAF, LEAF), (NEAR * LEAF) ** -0.5, 0.125, ((0, 256),)),
        "near_offset": draw_near_offset(jax.random.fold_in(arg_keys[12], 71), 0),
        "leaf_blocks": bell_draw(arg_keys[6], (LEAVES, KL, RANK, RANK), (KL * RANK) ** -0.5, 0.3125, ((0, 256),)),
        "leaf_partner": draw_leaf_partner(jax.random.fold_in(arg_keys[12], 71), 0),
        "leaf_count": draw_leaf_count(jax.random.fold_in(arg_keys[12], 71), 0),
        "top_blocks": bell_draw(arg_keys[9], (ROOTS, KT, RANK, RANK), (KT * RANK) ** -0.5, 0.125, ((0, 64), (1, 4))),
        "top_source": touch_ends(jax.random.randint(arg_keys[10], (ROOTS, KT), 0, ROOTS), jax.random.fold_in(arg_keys[10], 1), 0, ROOTS - 1).astype(jnp.int32),
        "top_count": draw_top_count(jax.random.fold_in(arg_keys[12], 71), 0),
    }


def neighbour_rows(table, offsets):
    rim = jnp.zeros((LEAF_DEV,) + table.shape[1:], table.dtype)
    padded = jnp.concatenate([rim, table, rim], axis=0)
    index = jnp.arange(LEAVES, dtype=jnp.int32) + offsets.astype(jnp.int32) + LEAF_DEV
    return jnp.take(padded, index.astype(jnp.int32), axis=0)


def reference(unknowns, leaf_basis, leaf_transfer, parent_transfer, near_blocks, near_offset, leaf_blocks, leaf_partner, leaf_count, top_blocks, top_source, top_count):
    high = lax.Precision.HIGHEST
    single = jnp.float32
    leaf_moment = jnp.einsum('glr,gln->grn', leaf_basis.astype(single), unknowns.astype(single), precision=high).astype(jnp.bfloat16)
    near_sum = jnp.zeros((LEAVES, LEAF, NRHS), single)
    for slot in range(NEAR):
        column_rows = neighbour_rows(unknowns, near_offset[:, slot])
        near_sum = near_sum + jnp.einsum('gab,gbn->gan', near_blocks[:, slot].astype(single), column_rows.astype(single), precision=high)
    leaf_far = jnp.zeros((LEAVES, RANK, NRHS), single)
    for slot in range(KL):
        source_rows = neighbour_rows(leaf_moment, leaf_partner[:, slot]).astype(single)
        live_mask = (leaf_count > slot).astype(single)
        leaf_far = leaf_far + live_mask[:, None, None] * jnp.einsum('gab,gbn->gan', leaf_blocks[:, slot].astype(single), source_rows, precision=high)
    child_transfer = leaf_transfer.reshape(PARENTS, LEAF_DEV, RANK, RANK).astype(single)
    child_moment = leaf_moment.reshape(PARENTS, LEAF_DEV, RANK, NRHS).astype(single)
    parent_moment = jnp.einsum('pkrs,pkrn->psn', child_transfer, child_moment, precision=high).astype(jnp.bfloat16)
    root_terms = jnp.einsum('prs,prn->psn', parent_transfer.astype(single), parent_moment.astype(single), precision=high)
    root_moment = jnp.sum(root_terms.reshape(ROOTS, N_LEVEL, RANK, NRHS), axis=1).astype(jnp.bfloat16)
    slot_live = (jnp.arange(KT, dtype=jnp.int32)[None, :] < top_count[:, None]).astype(single)
    picked = jnp.take(root_moment, top_source.astype(jnp.int32), axis=0).astype(single) * slot_live[:, :, None, None]
    root_field = jnp.einsum('tkab,tkbn->tan', top_blocks.astype(single), picked, precision=high)
    parent_field = jnp.einsum('prs,psn->prn', parent_transfer.astype(single), jnp.repeat(root_field, N_LEVEL, axis=0), precision=high)
    leaf_field = jnp.einsum('pkrs,psn->pkrn', child_transfer, parent_field, precision=high).reshape(LEAVES, RANK, NRHS) + leaf_far
    leaf_field = leaf_field.astype(jnp.bfloat16)
    return jnp.einsum('glr,grn->gln', leaf_basis.astype(single), leaf_field.astype(single), precision=high) + near_sum
```

```python
import functools

import jax
import jax.numpy as jnp
from jax import lax
from jax.experimental import pallas as pl
from jax.experimental.pallas import tpu as pltpu
from jax.sharding import PartitionSpec as P

X, Z, CORES = 4, 8, 2
LEVEL = 4
BF = jnp.bfloat16
F32 = jnp.float32
MIB = 1 << 20

OWN = (4, 5, 6, 7)
HALO = (0, 1, 2, 3, 8, 9, 10, 11)


def dot(a, b, dims=((1,), (0,))):
    return lax.dot_general(a, b, (dims, ((), ())), preferred_element_type=F32)


def near_block(slot_ref, nb_ref, target, place):
    slot = slot_ref[target, place - target]
    block = nb_ref[target, jnp.maximum(slot, 0)]
    return jnp.where(slot >= 0, block, jnp.zeros_like(block))


def moments_kernel(
    u_ref, bt_ref, lt_ref, pt_ref, tb_ref, msg_ref, out_ref, m_ref, u, bt, lt, pt, tb, sem, out_sem
):
    small = [
        pltpu.make_async_copy(src, dst, sem.at[4 + n])
        for n, (src, dst) in enumerate(((bt_ref, bt), (lt_ref, lt), (pt_ref, pt), (tb_ref, tb)))
    ]
    large = [pltpu.make_async_copy(u_ref.at[g], u.at[g], sem.at[g]) for g in range(4)]
    outward = [
        pltpu.make_async_copy(u.at[g], out_ref.at[256 * g : 256 * (g + 1)], out_sem.at[g]) for g in range(4)
    ]
    outward += [
        pltpu.make_async_copy(bt.at[g], out_ref.at[1024:1088, 256 * g : 256 * (g + 1)], out_sem.at[4 + g])
        for g in range(4)
    ]
    small[0].start()
    for copy in large + small[1:]:
        copy.start()
    small[0].wait()
    for g in range(4):
        outward[4 + g].start()
    for g in range(4):
        large[g].wait()
        outward[g].start()
        m_ref[64 * g : 64 * (g + 1)] = dot(bt[g], u[g]).astype(BF)
    for copy in small[1:]:
        copy.wait()
    parent = dot(lt[...], m_ref[...], ((0,), (0,))).astype(BF)
    packed = jnp.concatenate([pt[16 * j : 16 * (j + 1)] for j in range(4)], axis=1)
    blocks = [jnp.concatenate([tb[4 * half + s] for s in range(4)], axis=1) for half in range(2)]
    for q in range(LEVEL):
        msg_ref[q, 0:64] = parent[:, 256 * q : 256 * (q + 1)]
        msg_ref[q, 64:128] = blocks[0]
        msg_ref[q, 128:192] = blocks[1]
        msg_ref[q, 192:208] = packed
    for copy in outward:
        copy.wait()


def roots_kernel(msg_ref, after_ref, out_ref, held, sem):
    copies = [
        pltpu.make_async_copy(msg_ref.at[k, at : at + size], held.at[k, to : to + size], sem.at[k, n])
        for k in range(LEVEL)
        for n, (at, size, to) in enumerate(((0, 64, 0), (192, 16, 64)))
    ]
    for copy in copies:
        copy.start()
    for copy in copies:
        copy.wait()
    total = jnp.zeros((64, 256), F32)
    for k in range(LEVEL):
        packed = held[k, 64:80]
        pt = jnp.concatenate([packed[:, 64 * j : 64 * (j + 1)] for j in range(4)], axis=0)
        total += dot(pt, held[k, 0:64], ((0,), (0,)))
    root = total.astype(BF)
    for z in range(Z):
        out_ref[z] = root


def after_kernel(*refs):
    pass


def ordered(arrays, after, name):
    return pl.pallas_call(
        after_kernel,
        in_specs=[HBM] * (len(arrays) + len(after)),
        out_specs=[HBM] * len(arrays),
        out_shape=[jax.ShapeDtypeStruct(array.shape, array.dtype) for array in arrays],
        input_output_aliases={n: n for n in range(len(arrays))},
        compiler_params=params(60),
        name=name,
    )(*arrays, *after)


def crossing_kernel(u_ref, bt_ref, after_ref, out_ref, held, sem):
    rows = [(256 * g, 256) for g in range(4)] + [(1024, 64)]
    inward = [pltpu.make_async_copy(u_ref.at[g], held.at[256 * g : 256 * (g + 1)], sem.at[0, g]) for g in range(4)]
    inward += [
        pltpu.make_async_copy(bt_ref.at[g], held.at[1024:1088, 256 * g : 256 * (g + 1)], sem.at[0, 4 + g])
        for g in range(4)
    ]
    outward = [
        pltpu.make_async_copy(held.at[at : at + size], out_ref.at[at : at + size], sem.at[1, n])
        for n, (at, size) in enumerate(rows)
    ]
    for copy in inward:
        copy.start()
    for g in range(4):
        inward[g].wait()
        outward[g].start()
    for copy in inward[4:]:
        copy.wait()
    outward[4].start()
    for copy in outward:
        copy.wait()


def near_kernel(
    offset_ref, partner_ref, count_ref, u_hbm, nb_hbm, lb_hbm, bt_hbm, p_hbm, n_hbm,
    acc_out, blocks_out, left_out, slot_ref, far_slot, u, nb, lb, bt, p, n, blocks, left, acc, sem, out_sem,
):
    def load(src, dst, at):
        copy = pltpu.make_async_copy(src, dst, sem.at[at])
        copy.start()
        return copy

    small = [load(lb_hbm, lb, 0), load(bt_hbm, bt, 1)]
    small += [load(p_hbm.at[1024:1088], p.at[1024:1088], 2), load(n_hbm.at[1024:1088], n.at[1024:1088], 3)]
    tables = [load(nb_hbm.at[0], nb.at[0], 4)]
    large = [load(u_hbm, u, 8), load(p_hbm.at[0:1024], p.at[0:1024], 9), load(n_hbm.at[0:1024], n.at[0:1024], 10)]
    tables += [load(nb_hbm.at[i], nb.at[i], 4 + i) for i in range(1, 4)]
    for i in range(4):
        for o in range(9):
            slot_ref[i, o] = -1
            far_slot[i, o] = -1
        for s in range(8):
            slot_ref[i, offset_ref[i, s] + 4] = s
        for s in range(6):

            @pl.when(s < count_ref[i])
            def _():
                far_slot[i, partner_ref[i, s] + 4] = s

    for copy in small:
        copy.wait()
    zero = jnp.zeros((64, 64), BF)
    outward = []
    for i in range(4):
        rows = slice(256 * i, 256 * (i + 1))
        places = list(range(i, 4)) + list(range(8, i + 9)) + [w for w in OWN if w != i + 4]
        coupling = []
        for w in places:
            slot = far_slot[i, w - i]
            coupling.append(jnp.where(slot >= 0, lb[i, jnp.maximum(slot, 0)], zero))
        left_i = dot(bt[i].T, jnp.concatenate(coupling, axis=1)).astype(BF)
        left[rows] = left_i[:, 0:320]
        tables[i].wait()
        for k, w in enumerate(places):
            if w in OWN:
                other, at = bt[w - 4], 1280 + 256 * (w - 4)
            else:
                ref, g = (p, w) if w < 4 else (n, w - 8)
                other, at = ref[1024:1088, 256 * g : 256 * (g + 1)], 256 * k
            block = near_block(slot_ref, nb, i, w).astype(F32) + dot(left_i[:, 64 * k : 64 * (k + 1)], other)
            blocks[rows, at : at + 256] = block.astype(BF)
        blocks[rows, 1280 + 256 * i : 1536 + 256 * i] = near_block(slot_ref, nb, i, i + 4)
        if i == 0:
            for copy in large:
                copy.wait()
        for half in range(2):
            cols = slice(512 * half, 512 * (half + 1))
            sources = [p[256 * w : 256 * (w + 1), cols] for w in range(i, 4)]
            sources += [n[256 * w : 256 * (w + 1), cols] for w in range(i + 1)]
            sources += [u[w, :, cols] for w in range(4)]
            acc[i, :, cols] = dot(blocks[rows], jnp.concatenate(sources, axis=0))
        outward.append(pltpu.make_async_copy(acc.at[i], acc_out.at[i], out_sem.at[i]))
        outward[-1].start()
    outward.append(pltpu.make_async_copy(blocks.at[:, 0:1280], blocks_out, out_sem.at[4]))
    outward[-1].start()
    outward.append(pltpu.make_async_copy(left, left_out, out_sem.at[5]))
    outward[-1].start()
    for copy in outward:
        copy.wait()


def top_kernel(source_ref, count_ref, own0, own1, own2, own3, other0, other1, other2, other3, msg_ref, out_ref, table, blocks, sem, block_sem):
    copies = []
    for k, pair in enumerate(((own0, other0), (own1, other1), (own2, other2), (own3, other3))):
        for c in range(CORES):
            copies.append(pltpu.make_async_copy(pair[c], table.at[c, k], sem.at[c, k]))
    for k in range(LEVEL):
        copies.append(pltpu.make_async_copy(msg_ref.at[k, 64:192], blocks.at[k], block_sem.at[k]))
    for copy in copies:
        copy.start()
    for copy in copies:
        copy.wait()
    lead = lax.axis_index("leaf")
    my_x, my_core = lead // (Z * CORES), lax.rem(lead, CORES)
    total = jnp.zeros((64, 256), F32)
    for k in range(LEVEL):
        for half in range(2):
            rows = []
            for s in range(4):
                at = 8 * k + 4 * half + s
                source = source_ref[0, at]
                core = lax.rem(source + my_core, CORES)
                step = lax.rem(my_x - source // (Z * CORES) + X, X)
                row = table[core, step, lax.rem(source // CORES, Z)]
                rows.append(jnp.where(at < count_ref[0], row, jnp.zeros_like(row)))
            total += dot(blocks[k, 64 * half : 64 * (half + 1)], jnp.concatenate(rows, axis=0))
    for k in range(LEVEL):
        out_ref[k] = total.astype(BF)


def last_kernel(
    cross_hbm, blocks_hbm, left_hbm, acc_hbm, field_hbm, lt_hbm, pt_hbm, bt_hbm, out_ref,
    cross, blocks, left, acc, field, lt, pt, bt, held, sem, out_sem,
):
    def load(src, dst, at):
        return pltpu.make_async_copy(src, dst, sem.at[at])

    small = [load(field_hbm, field, 0), load(lt_hbm, lt, 1), load(pt_hbm, pt, 2), load(bt_hbm, bt, 3)]
    large = [load(acc_hbm.at[i], acc.at[i], 4 + i) for i in range(4)]
    extra = [load(left_hbm, left, 8), load(blocks_hbm, blocks, 9), load(cross_hbm, cross, 10)]
    level = lax.axis_index("level")
    core = lax.rem(lax.axis_index("leaf"), CORES)
    cross_prev = jnp.logical_and(level == 0, core == 0)
    cross_next = jnp.logical_and(level == LEVEL - 1, core == CORES - 1)
    leaf_rows = [slice(256 * w, 256 * (w + 1)) for w in range(4)]
    sides = ((cross_prev, lambda i: range(0, 4 - i)), (cross_next, lambda i: range(4 - i, 5)))
    crossing = jnp.logical_or(cross_prev, cross_next)

    for copy in small + large:
        copy.start()

    @pl.when(crossing)
    def _():
        for copy in extra:
            copy.start()
        for copy in extra:
            copy.wait()

    for side, places in sides:

        @pl.when(side)
        def _():
            for i in range(4):
                target = leaf_rows[i]
                for n in places(i):
                    far = dot(left[target, 64 * n : 64 * (n + 1)], cross[1024:1088, leaf_rows[(i + n) % 4]])
                    block = blocks[target, 256 * n : 256 * (n + 1)].astype(F32) + far
                    blocks[target, 256 * n : 256 * (n + 1)] = block.astype(BF)

    for copy in small:
        copy.wait()
    whole = jnp.concatenate([field[q] for q in range(LEVEL)], axis=1)
    parent = dot(pt[...], whole)
    high = parent.astype(BF)
    low = (parent - high.astype(F32)).astype(BF)
    outward = []
    for i in range(4):
        basis = bt[i].T
        transfer = lt[64 * i : 64 * (i + 1)]
        leaf = dot(transfer, high) + dot(transfer, low)
        leaf_high = leaf.astype(BF)
        leaf_low = (leaf - leaf_high.astype(F32)).astype(BF)
        large[i].wait()
        held[i] = acc[i] + dot(
            jnp.concatenate([basis, basis], axis=1), jnp.concatenate([leaf_high, leaf_low], axis=0)
        )

        for side, places in sides:

            @pl.when(side)
            def _():
                reach = places(i)
                sources = [cross[leaf_rows[(i + n) % 4]] for n in reach]
                held[i] += dot(
                    blocks[leaf_rows[i], 256 * reach[0] : 256 * (reach[-1] + 1)], jnp.concatenate(sources, axis=0)
                )

        outward.append(pltpu.make_async_copy(held.at[i], out_ref.at[i], out_sem.at[i]))
        outward[-1].start()
    for copy in outward:
        copy.wait()


def params(mib):
    return pltpu.CompilerParams(vmem_limit_bytes=mib * MIB)


VMEM = pl.BlockSpec(memory_space=pltpu.VMEM)
SMEM = pl.BlockSpec(memory_space=pltpu.SMEM)
ANY = pl.BlockSpec(memory_space=pl.ANY)
HBM = pl.BlockSpec(memory_space=pltpu.HBM)


def body(
    unknowns, leaf_basis, leaf_transfer, parent_transfer, near_blocks, near_offset,
    leaf_blocks, leaf_partner, leaf_count, top_blocks, top_source, top_count,
):
    both = ("leaf", "level")
    total = lax.axis_size("leaf") * LEVEL
    ahead = [(i, i + 1) for i in range(total - 1)]
    back = [(i + 1, i) for i in range(total - 1)]

    def crossing(a):
        return a % LEVEL == LEVEL - 1 and a // LEVEL % CORES == CORES - 1

    bt = leaf_basis.transpose(0, 2, 1)
    lt = leaf_transfer.reshape(256, 64)
    pt = parent_transfer[0]

    pieces, message = pl.pallas_call(
        moments_kernel,
        in_specs=[HBM] * 5,
        out_specs=[VMEM, HBM],
        out_shape=[jax.ShapeDtypeStruct((LEVEL, 208, 256), BF), jax.ShapeDtypeStruct((1088, 1024), BF)],
        scratch_shapes=[
            pltpu.VMEM((256, 1024), BF), pltpu.VMEM((4, 256, 1024), BF), pltpu.VMEM((4, 64, 256), BF),
            pltpu.VMEM((256, 64), BF), pltpu.VMEM((64, 64), BF), pltpu.VMEM((8, 64, 64), BF),
            pltpu.SemaphoreType.DMA((8,)), pltpu.SemaphoreType.DMA((8,)),
        ],
        compiler_params=params(60),
        name="moments",
    )(unknowns, bt, lt, pt, top_blocks[0])

    heap = lax.all_to_all(pieces, "level", 0, 0, tiled=True)

    (message,) = ordered([message], [heap], "send_inner")
    inner = lambda pairs: [(a, b) for a, b in pairs if not crossing(min(a, b))]
    inner_prev = lax.ppermute(message, both, inner(ahead))
    inner_next = lax.ppermute(message, both, inner(back))

    root = pl.pallas_call(
        roots_kernel,
        in_specs=[HBM] * 2,
        out_specs=VMEM,
        out_shape=jax.ShapeDtypeStruct((Z, 64, 256), BF),
        scratch_shapes=[pltpu.VMEM((LEVEL, 80, 256), BF), pltpu.SemaphoreType.DMA((LEVEL, 2))],
        compiler_params=params(60),
        name="roots",
    )(heap, message)

    def place(x, z, c):
        return (x * Z + z) * CORES + c

    leaves = [(x, z, c) for x in range(X) for z in range(Z) for c in range(CORES)]
    along_x = lambda step: [(place(x, z, c), place((x + step) % X, z, c)) for x, z, c in leaves]
    swap = [(place(x, z, c), place(x, z, 1 - c)) for x, z, c in leaves]
    groups = [[place(x, z, c) for z in range(Z)] for x in range(X) for c in range(CORES)]
    column = lax.all_to_all(root, "leaf", 0, 0, axis_index_groups=groups, tiled=True)
    mine = [column] + [lax.ppermute(column, "leaf", along_x(step)) for step in range(1, X)]
    theirs = [lax.ppermute(m, "leaf", swap) for m in mine]
    acc_shape = jax.ShapeDtypeStruct((4, 256, 1024), F32)
    message = pl.pallas_call(
        crossing_kernel,
        in_specs=[HBM] * 3,
        out_specs=HBM,
        out_shape=jax.ShapeDtypeStruct((1088, 1024), BF),
        scratch_shapes=[pltpu.VMEM((1088, 1024), BF), pltpu.SemaphoreType.DMA((2, 8))],
        compiler_params=params(60),
        name="send_crossing",
    )(unknowns, bt, mine[1])
    cross = lax.ppermute(message, both, [(a, b) for a, b in ahead + back if crossing(min(a, b))])

    field = pl.pallas_call(
        top_kernel,
        in_specs=[SMEM, SMEM] + [HBM] * 9,
        out_specs=VMEM,
        scratch_shapes=[
            pltpu.VMEM((CORES, X, Z, 64, 256), BF), pltpu.VMEM((LEVEL, 128, 256), BF),
            pltpu.SemaphoreType.DMA((CORES, X)), pltpu.SemaphoreType.DMA((LEVEL,)),
        ],
        out_shape=jax.ShapeDtypeStruct((LEVEL, 64, 256), BF),
        compiler_params=params(60),
        name="top",
    )(top_source, top_count, *mine, *theirs, heap)
    fields = lax.all_to_all(field, "level", 0, 0, tiled=True)

    acc, blocks, left = pl.pallas_call(
        near_kernel,
        in_specs=[SMEM] * 3 + [HBM] * 6,
        out_specs=[HBM] * 3,
        out_shape=[
            acc_shape, jax.ShapeDtypeStruct((1024, 1280), BF), jax.ShapeDtypeStruct((1024, 320), BF),
        ],
        scratch_shapes=[
            pltpu.SMEM((4, 9), jnp.int32), pltpu.SMEM((4, 9), jnp.int32), pltpu.VMEM((4, 256, 1024), BF),
            pltpu.VMEM((4, 8, 256, 256), BF), pltpu.VMEM((4, 6, 64, 64), BF), pltpu.VMEM((4, 64, 256), BF),
            pltpu.VMEM((1088, 1024), BF), pltpu.VMEM((1088, 1024), BF), pltpu.VMEM((1024, 2304), BF),
            pltpu.VMEM((1024, 320), BF), pltpu.VMEM((4, 256, 1024), F32),
            pltpu.SemaphoreType.DMA((11,)), pltpu.SemaphoreType.DMA((6,)),
        ],
        compiler_params=params(60),
        cost_estimate=pl.CostEstimate(flops=20_000_000_000, bytes_accessed=16 * MIB, transcendentals=0),
        name="near",
    )(near_offset, leaf_partner, leaf_count, unknowns, near_blocks, leaf_blocks, bt, inner_prev, inner_next)

    return pl.pallas_call(
        last_kernel,
        in_specs=[HBM] * 8,
        out_specs=HBM,
        out_shape=acc_shape,
        scratch_shapes=[
            pltpu.VMEM((1088, 1024), BF), pltpu.VMEM((1024, 1280), BF), pltpu.VMEM((1024, 320), BF),
            pltpu.VMEM((4, 256, 1024), F32), pltpu.VMEM((LEVEL, 64, 256), BF), pltpu.VMEM((256, 64), BF),
            pltpu.VMEM((64, 64), BF), pltpu.VMEM((4, 64, 256), BF), pltpu.VMEM((4, 256, 1024), F32),
            pltpu.SemaphoreType.DMA((11,)), pltpu.SemaphoreType.DMA((4,)),
        ],
        compiler_params=params(60),
        name="product",
    )(cross, blocks, left, acc, fields, lt, pt, bt)


def solution(mesh):
    return jax.shard_map(
        body,
        mesh=mesh,
        in_specs=(
            P(("leaf", "level"), None, None),
            P(("leaf", "level"), None, None),
            P(("leaf", "level"), None, None),
            P(("leaf", "level"), None, None),
            P(("leaf", "level"), None, None, None),
            P(("leaf", "level"), None),
            P(("leaf", "level"), None, None, None),
            P(("leaf", "level"), None),
            P(("leaf", "level")),
            P("leaf", "level", None, None),
            P("leaf", None),
            P("leaf"),
        ),
        out_specs=P(("leaf", "level"), None, None),
        check_vma=False,
    )
```

```python
import functools

import jax
import jax.numpy as jnp
from jax import lax
from jax.experimental import pallas as pl
from jax.experimental.pallas import tpu as pltpu
from jax.sharding import PartitionSpec as P

X, Z, CORES = 4, 8, 2
LEVEL = 4
BF = jnp.bfloat16
F32 = jnp.float32
MIB = 1 << 20

OWN = (4, 5, 6, 7)
HALO = (0, 1, 2, 3, 8, 9, 10, 11)


def dot(a, b, dims=((1,), (0,))):
    return lax.dot_general(a, b, (dims, ((), ())), preferred_element_type=F32)


def near_block(slot_ref, nb_ref, target, place):
    slot = slot_ref[target, place - target]
    block = nb_ref[target, jnp.maximum(slot, 0)]
    return jnp.where(slot >= 0, block, jnp.zeros_like(block))


def moments_kernel(
    u_ref, bt_ref, lt_ref, pt_ref, tb_ref, msg_ref, out_ref, m_ref, u, bt, lt, pt, tb, sem, out_sem
):
    small = [
        pltpu.make_async_copy(src, dst, sem.at[4 + n])
        for n, (src, dst) in enumerate(((bt_ref, bt), (lt_ref, lt), (pt_ref, pt), (tb_ref, tb)))
    ]
    large = [pltpu.make_async_copy(u_ref.at[g], u.at[g], sem.at[g]) for g in range(4)]
    units, bases = [], []
    for n, ref in enumerate((out_ref,)):
        for g in range(4):
            rows = slice(256 * g, 256 * (g + 1))
            units.append(pltpu.make_async_copy(u.at[g], ref.at[rows], out_sem.at[n, g]))
            bases.append(pltpu.make_async_copy(bt.at[g], ref.at[1024:1088, rows], out_sem.at[n, 4 + g]))
    small[0].start()
    for copy in large + small[1:]:
        copy.start()
    small[0].wait()
    for copy in bases:
        copy.start()
    for g in range(4):
        large[g].wait()
        units[g].start()
        m_ref[64 * g : 64 * (g + 1)] = dot(bt[g], u[g]).astype(BF)
    for copy in small[1:]:
        copy.wait()
    parent = dot(lt[...], m_ref[...], ((0,), (0,))).astype(BF)
    packed = jnp.concatenate([pt[16 * j : 16 * (j + 1)] for j in range(4)], axis=1)
    blocks = [jnp.concatenate([tb[4 * half + s] for s in range(4)], axis=1) for half in range(2)]
    for q in range(LEVEL):
        msg_ref[q, 0:64] = parent[:, 256 * q : 256 * (q + 1)]
        msg_ref[q, 64:128] = blocks[0]
        msg_ref[q, 128:192] = blocks[1]
        msg_ref[q, 192:208] = packed
    for copy in units + bases:
        copy.wait()


def roots_kernel(msg_ref, after_ref, out_ref, held, sem):
    copies = [
        pltpu.make_async_copy(msg_ref.at[k, at : at + size], held.at[k, to : to + size], sem.at[k, n])
        for k in range(LEVEL)
        for n, (at, size, to) in enumerate(((0, 64, 0), (192, 16, 64)))
    ]
    for copy in copies:
        copy.start()
    for copy in copies:
        copy.wait()
    total = jnp.zeros((64, 256), F32)
    for k in range(LEVEL):
        packed = held[k, 64:80]
        pt = jnp.concatenate([packed[:, 64 * j : 64 * (j + 1)] for j in range(4)], axis=0)
        total += dot(pt, held[k, 0:64], ((0,), (0,)))
    root = total.astype(BF)
    for z in range(Z):
        out_ref[z] = root


def after_kernel(*refs):
    pass


def ordered(arrays, after, name, **options):
    return pl.pallas_call(
        after_kernel,
        in_specs=[HBM] * (len(arrays) + len(after)),
        out_specs=[HBM] * len(arrays),
        out_shape=[jax.ShapeDtypeStruct(array.shape, array.dtype) for array in arrays],
        input_output_aliases={n: n for n in range(len(arrays))},
        compiler_params=params(60),
        name=name,
        **options,
    )(*arrays, *after)


def own_kernel(
    offset_ref, partner_ref, count_ref, u_hbm, nb_hbm, lb_hbm, bt_hbm, after_ref,
    acc_out, blocks_out, left_out, cross_out, far_out, slot_ref, far_slot, u, nb, lb, bt, own, blocks, left, acc,
    sem, out_sem, halo_sem,
):
    def load(src, dst, at):
        copy = pltpu.make_async_copy(src, dst, sem.at[at])
        copy.start()
        return copy

    small = [load(lb_hbm, lb, 0), load(bt_hbm, bt, 1)]
    tables = [load(nb_hbm.at[0], nb.at[0], 2)]
    units = load(u_hbm, u, 6)
    tables += [load(nb_hbm.at[i], nb.at[i], 2 + i) for i in range(1, 4)]
    for i in range(4):
        for o in range(9):
            slot_ref[i, o] = -1
            far_slot[i, o] = -1
        for s in range(8):
            slot_ref[i, offset_ref[i, s] + 4] = s
        for s in range(6):

            @pl.when(s < count_ref[i])
            def _():
                far_slot[i, partner_ref[i, s] + 4] = s

    for copy in small:
        copy.wait()
    zero = jnp.zeros((64, 64), BF)
    outward = []
    for n, ref in enumerate((cross_out, far_out)):
        for g in range(4):
            cols = slice(256 * g, 256 * (g + 1))
            outward.append(pltpu.make_async_copy(bt.at[g], ref.at[1024:1088, cols], halo_sem.at[n, 4 + g]))
            outward[-1].start()
    for i in range(4):
        rows = slice(256 * i, 256 * (i + 1))
        places = list(range(i, 4)) + list(range(8, i + 9)) + [w for w in OWN if w != i + 4]
        coupling = []
        for w in places:
            slot = far_slot[i, w - i]
            coupling.append(jnp.where(slot >= 0, lb[i, jnp.maximum(slot, 0)], zero))
        left_i = dot(bt[i].T, jnp.concatenate(coupling, axis=1)).astype(BF)
        left[rows] = left_i[:, 0:320]
        tables[i].wait()
        for k, w in enumerate(places):
            block = near_block(slot_ref, nb, i, w)
            if w in OWN:
                block = block.astype(F32) + dot(left_i[:, 64 * k : 64 * (k + 1)], bt[w - 4])
                own[:, 256 * (w - 4) : 256 * (w - 3)] = block.astype(BF)
            else:
                blocks[rows, 256 * k : 256 * (k + 1)] = block
        own[:, rows] = near_block(slot_ref, nb, i, i + 4)
        outward.append(pltpu.make_async_copy(blocks.at[rows], blocks_out.at[rows], out_sem.at[i]))
        outward[-1].start()
        if i == 0:
            units.wait()
            for n, ref in enumerate((cross_out, far_out)):
                for g in range(4):
                    copy = pltpu.make_async_copy(u.at[g], ref.at[256 * g : 256 * (g + 1)], halo_sem.at[n, g])
                    copy.start()
                    outward.append(copy)
        for half in range(2):
            cols = slice(512 * half, 512 * (half + 1))
            acc[i, :, cols] = dot(own[...], jnp.concatenate([u[w, :, cols] for w in range(4)], axis=0))
        outward.append(pltpu.make_async_copy(acc.at[i], acc_out.at[i], out_sem.at[4 + i]))
        outward[-1].start()
    outward.append(pltpu.make_async_copy(left, left_out, out_sem.at[8]))
    outward[-1].start()
    for copy in outward:
        copy.wait()


def folded(blocks, left, i, k, basis):
    rows = slice(256 * i, 256 * (i + 1))
    far = dot(left[rows, 64 * k : 64 * (k + 1)], basis)
    return (blocks[rows, 256 * k : 256 * (k + 1)].astype(F32) + far).astype(BF)


def top_kernel(source_ref, count_ref, own0, own1, own2, own3, other0, other1, other2, other3, msg_ref, after_ref, out_ref, table, blocks, sem, block_sem):
    copies = []
    for k, pair in enumerate(((own0, other0), (own1, other1), (own2, other2), (own3, other3))):
        for c in range(CORES):
            copies.append(pltpu.make_async_copy(pair[c], table.at[c, k], sem.at[c, k]))
    for k in range(LEVEL):
        copies.append(pltpu.make_async_copy(msg_ref.at[k, 64:192], blocks.at[k], block_sem.at[k]))
    for copy in copies:
        copy.start()
    for copy in copies:
        copy.wait()
    lead = lax.axis_index("leaf")
    my_x, my_core = lead // (Z * CORES), lax.rem(lead, CORES)
    total = jnp.zeros((64, 256), F32)
    for k in range(LEVEL):
        for half in range(2):
            rows = []
            for s in range(4):
                at = 8 * k + 4 * half + s
                source = source_ref[0, at]
                core = lax.rem(source + my_core, CORES)
                step = lax.rem(my_x - source // (Z * CORES) + X, X)
                row = table[core, step, lax.rem(source // CORES, Z)]
                rows.append(jnp.where(at < count_ref[0], row, jnp.zeros_like(row)))
            total += dot(blocks[k, 64 * half : 64 * (half + 1)], jnp.concatenate(rows, axis=0))
    for k in range(LEVEL):
        out_ref[k] = total.astype(BF)


def last_kernel(
    p_hbm, n_hbm, cross_hbm, far_hbm, blocks_hbm, left_hbm, acc_hbm, field_hbm, lt_hbm, pt_hbm, bt_hbm, out_ref,
    p, n, blocks, left, acc, field, lt, pt, bt, row, held, sem, side_sem, out_sem,
):
    def load(src, dst, at):
        copy = pltpu.make_async_copy(src, dst, sem.at[at])
        copy.start()
        return copy

    lead, level = lax.axis_index("leaf"), lax.axis_index("level")
    core, z = lax.rem(lead, CORES), lax.rem(lead // CORES, Z)
    cross_prev = jnp.logical_and(level == 0, core == 0)
    cross_next = jnp.logical_and(level == LEVEL - 1, core == CORES - 1)
    sides = []
    for n_side, (dst, inner, crossed, end) in enumerate(((p, p_hbm, cross_prev, 0), (n, n_hbm, cross_next, Z - 1))):
        near = [
            pltpu.make_async_copy(inner.at[at : at + size], dst.at[at : at + size], side_sem.at[n_side, m])
            for m, (at, size) in enumerate(((1024, 64), (0, 1024)))
        ]
        cases = [(inner, jnp.logical_not(crossed))]
        cases += [(cross_hbm, jnp.logical_and(crossed, z != end)), (far_hbm, jnp.logical_and(crossed, z == end))]
        for src, here in cases:

            @pl.when(here)
            def _():
                for m, (at, size) in enumerate(((1024, 64), (0, 1024))):
                    pltpu.make_async_copy(
                        src.at[at : at + size], dst.at[at : at + size], side_sem.at[n_side, m]
                    ).start()

        sides.append(near)
    small = [load(left_hbm, left, 0), load(field_hbm, field, 1), load(lt_hbm, lt, 2), load(pt_hbm, pt, 3)]
    small.append(load(bt_hbm, bt, 4))
    tables, sums = [], []
    for i in range(4):
        rows = slice(256 * i, 256 * (i + 1))
        tables.append(load(blocks_hbm.at[rows], blocks.at[rows], 5 + i))
        sums.append(load(acc_hbm.at[i], acc.at[i], 9 + i))

    for copy in small + [sides[0][0], sides[1][0]]:
        copy.wait()
    parent = dot(pt[...], jnp.concatenate([field[q] for q in range(LEVEL)], axis=1))
    high = parent.astype(BF)
    low = (parent - high.astype(F32)).astype(BF)
    outward = []
    for i in range(4):
        basis = bt[i].T
        transfer = lt[64 * i : 64 * (i + 1)]
        leaf = dot(transfer, high) + dot(transfer, low)
        leaf_high = leaf.astype(BF)
        leaf_low = (leaf - leaf_high.astype(F32)).astype(BF)
        tables[i].wait()
        for k in range(5):
            ref, g = (p, i + k) if i + k < 4 else (n, i + k - 4)
            row[:, 256 * k : 256 * (k + 1)] = folded(blocks, left, i, k, ref[1024:1088, 256 * g : 256 * (g + 1)])
        row[:, 1280:1408] = jnp.concatenate([basis, basis], axis=1)
        if i == 0:
            sides[0][1].wait()
            sides[1][1].wait()
        sums[i].wait()
        for half in range(2):
            cols = slice(512 * half, 512 * (half + 1))
            sources = [p[256 * w : 256 * (w + 1), cols] for w in range(i, 4)]
            sources += [n[256 * w : 256 * (w + 1), cols] for w in range(i + 1)]
            sources += [leaf_high[:, cols], leaf_low[:, cols]]
            held[i, :, cols] = acc[i, :, cols] + dot(row[...], jnp.concatenate(sources, axis=0))
        outward.append(pltpu.make_async_copy(held.at[i], out_ref.at[i], out_sem.at[i]))
        outward[-1].start()
    for copy in outward:
        copy.wait()


def params(mib):
    return pltpu.CompilerParams(vmem_limit_bytes=mib * MIB)


VMEM = pl.BlockSpec(memory_space=pltpu.VMEM)
SMEM = pl.BlockSpec(memory_space=pltpu.SMEM)
ANY = pl.BlockSpec(memory_space=pl.ANY)
HBM = pl.BlockSpec(memory_space=pltpu.HBM)


def body(
    unknowns, leaf_basis, leaf_transfer, parent_transfer, near_blocks, near_offset,
    leaf_blocks, leaf_partner, leaf_count, top_blocks, top_source, top_count,
):
    both = ("leaf", "level")
    total = lax.axis_size("leaf") * LEVEL
    ahead = [(i, i + 1) for i in range(total - 1)]
    back = [(i + 1, i) for i in range(total - 1)]

    def crossing(a):
        return a % LEVEL == LEVEL - 1 and a // LEVEL % CORES == CORES - 1

    bt = leaf_basis.transpose(0, 2, 1)
    lt = leaf_transfer.reshape(256, 64)
    pt = parent_transfer[0]

    pieces, message = pl.pallas_call(
        moments_kernel,
        in_specs=[HBM] * 5,
        out_specs=[VMEM, HBM],
        out_shape=[jax.ShapeDtypeStruct((LEVEL, 208, 256), BF)] + [jax.ShapeDtypeStruct((1088, 1024), BF)],
        scratch_shapes=[
            pltpu.VMEM((256, 1024), BF), pltpu.VMEM((4, 256, 1024), BF), pltpu.VMEM((4, 64, 256), BF),
            pltpu.VMEM((256, 64), BF), pltpu.VMEM((64, 64), BF), pltpu.VMEM((8, 64, 64), BF),
            pltpu.SemaphoreType.DMA((8,)), pltpu.SemaphoreType.DMA((1, 8)),
        ],
        compiler_params=params(60),
        name="moments",
    )(unknowns, bt, lt, pt, top_blocks[0])

    heap = lax.all_to_all(pieces, "level", 0, 0, tiled=True)

    (message,) = ordered([message], [heap], "send_inner")
    inner = lambda pairs: [(a, b) for a, b in pairs if not crossing(min(a, b))]
    inner_prev = lax.ppermute(message, both, inner(ahead))
    inner_next = lax.ppermute(message, both, inner(back))

    root = pl.pallas_call(
        roots_kernel,
        in_specs=[HBM] * 2,
        out_specs=VMEM,
        out_shape=jax.ShapeDtypeStruct((Z, 64, 256), BF),
        scratch_shapes=[pltpu.VMEM((LEVEL, 80, 256), BF), pltpu.SemaphoreType.DMA((LEVEL, 2))],
        compiler_params=params(60),
        name="roots",
    )(heap, message)

    def place(x, z, c):
        return (x * Z + z) * CORES + c

    leaves = [(x, z, c) for x in range(X) for z in range(Z) for c in range(CORES)]
    along_x = lambda step: [(place(x, z, c), place((x + step) % X, z, c)) for x, z, c in leaves]
    swap = [(place(x, z, c), place(x, z, 1 - c)) for x, z, c in leaves]
    groups = [[place(x, z, c) for z in range(Z)] for x in range(X) for c in range(CORES)]
    column = lax.all_to_all(root, "leaf", 0, 0, axis_index_groups=groups, tiled=True)
    chips = [(a, b) for a, b in ahead + back if crossing(min(a, b))]
    along_row = lambda a: a // (LEVEL * CORES) % Z == Z - 1
    acc_shape = jax.ShapeDtypeStruct((4, 256, 1024), F32)
    acc, blocks, left, cross_message, far_message = pl.pallas_call(
        own_kernel,
        in_specs=[SMEM] * 3 + [HBM] * 5,
        out_specs=[HBM] * 5,
        out_shape=[
            acc_shape, jax.ShapeDtypeStruct((1024, 1280), BF), jax.ShapeDtypeStruct((1024, 320), BF),
        ]
        + [jax.ShapeDtypeStruct((1088, 1024), BF)] * 2,
        scratch_shapes=[
            pltpu.SMEM((4, 9), jnp.int32), pltpu.SMEM((4, 9), jnp.int32), pltpu.VMEM((4, 256, 1024), BF),
            pltpu.VMEM((4, 8, 256, 256), BF), pltpu.VMEM((4, 6, 64, 64), BF), pltpu.VMEM((4, 64, 256), BF),
            pltpu.VMEM((256, 1024), BF), pltpu.VMEM((1024, 1280), BF), pltpu.VMEM((1024, 320), BF),
            pltpu.VMEM((4, 256, 1024), F32), pltpu.SemaphoreType.DMA((7,)), pltpu.SemaphoreType.DMA((9,)),
            pltpu.SemaphoreType.DMA((2, 8)),
        ],
        compiler_params=params(60),
        cost_estimate=pl.CostEstimate(flops=6_000_000_000, bytes_accessed=16 * MIB, transcendentals=0),
        name="near_own",
    )(near_offset, leaf_partner, leaf_count, unknowns, near_blocks, leaf_blocks, bt, column)

    cross = lax.ppermute(cross_message, both, [pair for pair in chips if not along_row(min(pair))])
    mine = [lax.ppermute(column, "leaf", along_x(step)) for step in range(1, X)]
    mine = [column] + list(ordered(mine, [left], "gathered"))
    theirs = [lax.ppermute(m, "leaf", swap) for m in mine]
    (far_message,) = ordered([far_message], [mine[1]], "send_far")
    far_cross = lax.ppermute(far_message, both, [pair for pair in chips if along_row(min(pair))])

    field = pl.pallas_call(
        top_kernel,
        in_specs=[SMEM, SMEM] + [HBM] * 10,
        out_specs=VMEM,
        scratch_shapes=[
            pltpu.VMEM((CORES, X, Z, 64, 256), BF), pltpu.VMEM((LEVEL, 128, 256), BF),
            pltpu.SemaphoreType.DMA((CORES, X)), pltpu.SemaphoreType.DMA((LEVEL,)),
        ],
        out_shape=jax.ShapeDtypeStruct((LEVEL, 64, 256), BF),
        compiler_params=params(60),
        name="top",
    )(top_source, top_count, *mine, *theirs, heap, left)
    fields = lax.all_to_all(field, "level", 0, 0, tiled=True)

    inner_prev, inner_next = ordered(
        [inner_prev, inner_next], [left], "arrived",
        cost_estimate=pl.CostEstimate(flops=8_000_000_000, bytes_accessed=16 * MIB, transcendentals=0),
    )
    return pl.pallas_call(
        last_kernel,
        in_specs=[HBM] * 11,
        out_specs=HBM,
        out_shape=acc_shape,
        scratch_shapes=[
            pltpu.VMEM((1088, 1024), BF), pltpu.VMEM((1088, 1024), BF), pltpu.VMEM((1024, 1280), BF),
            pltpu.VMEM((1024, 320), BF), pltpu.VMEM((4, 256, 1024), F32), pltpu.VMEM((LEVEL, 64, 256), BF),
            pltpu.VMEM((256, 64), BF), pltpu.VMEM((64, 64), BF), pltpu.VMEM((4, 64, 256), BF),
            pltpu.VMEM((256, 1408), BF), pltpu.VMEM((4, 256, 1024), F32),
            pltpu.SemaphoreType.DMA((13,)), pltpu.SemaphoreType.DMA((2, 2)), pltpu.SemaphoreType.DMA((4,)),
        ],
        compiler_params=params(60),
        name="product",
    )(inner_prev, inner_next, cross, far_cross, blocks, left, acc, fields, lt, pt, bt)


def solution(mesh):
    return jax.shard_map(
        body,
        mesh=mesh,
        in_specs=(
            P(("leaf", "level"), None, None),
            P(("leaf", "level"), None, None),
            P(("leaf", "level"), None, None),
            P(("leaf", "level"), None, None),
            P(("leaf", "level"), None, None, None),
            P(("leaf", "level"), None),
            P(("leaf", "level"), None, None, None),
            P(("leaf", "level"), None),
            P(("leaf", "level")),
            P("leaf", "level", None, None),
            P("leaf", None),
            P("leaf"),
        ),
        out_specs=P(("leaf", "level"), None, None),
        check_vma=False,
    )
```

```python
import functools

import jax
import jax.numpy as jnp
from jax import lax
from jax.experimental import pallas as pl
from jax.experimental.pallas import tpu as pltpu
from jax.sharding import PartitionSpec as P

X, Z, CORES = 4, 8, 2
LEVEL = 4
BF = jnp.bfloat16
F32 = jnp.float32
MIB = 1 << 20

OWN = (4, 5, 6, 7)
HALO = (0, 1, 2, 3, 8, 9, 10, 11)


def dot(a, b, dims=((1,), (0,))):
    return lax.dot_general(a, b, (dims, ((), ())), preferred_element_type=F32)


def near_block(slot_ref, nb_ref, target, place):
    slot = slot_ref[target, place - target]
    block = nb_ref[target, jnp.maximum(slot, 0)]
    return jnp.where(slot >= 0, block, jnp.zeros_like(block))


def moments_kernel(
    u_ref, bt_ref, lt_ref, pt_ref, tb_ref, msg_ref, out_ref, m_ref, u, bt, lt, pt, tb, sem, out_sem
):
    small = [
        pltpu.make_async_copy(src, dst, sem.at[4 + n])
        for n, (src, dst) in enumerate(((bt_ref, bt), (lt_ref, lt), (pt_ref, pt), (tb_ref, tb)))
    ]
    large = [pltpu.make_async_copy(u_ref.at[g], u.at[g], sem.at[g]) for g in range(4)]
    units, bases = [], []
    for n, ref in enumerate((out_ref,)):
        for g in range(4):
            rows = slice(256 * g, 256 * (g + 1))
            units.append(pltpu.make_async_copy(u.at[g], ref.at[rows], out_sem.at[n, g]))
            bases.append(pltpu.make_async_copy(bt.at[g], ref.at[1024:1088, rows], out_sem.at[n, 4 + g]))
    small[0].start()
    for copy in large + small[1:]:
        copy.start()
    small[0].wait()
    for copy in bases:
        copy.start()
    for g in range(4):
        large[g].wait()
        units[g].start()
        m_ref[64 * g : 64 * (g + 1)] = dot(bt[g], u[g]).astype(BF)
    for copy in small[1:]:
        copy.wait()
    parent = dot(lt[...], m_ref[...], ((0,), (0,))).astype(BF)
    packed = jnp.concatenate([pt[16 * j : 16 * (j + 1)] for j in range(4)], axis=1)
    blocks = [jnp.concatenate([tb[4 * half + s] for s in range(4)], axis=1) for half in range(2)]
    for q in range(LEVEL):
        msg_ref[q, 0:64] = parent[:, 256 * q : 256 * (q + 1)]
        msg_ref[q, 64:80] = packed
        msg_ref[q, 80:144] = blocks[0]
        msg_ref[q, 144:208] = blocks[1]
    for copy in units + bases:
        copy.wait()


def roots_kernel(msg_ref, after_ref, out_ref, held, sem):
    copy = pltpu.make_async_copy(msg_ref.at[:, 0:80], held, sem)
    copy.start()
    copy.wait()
    total = jnp.zeros((64, 256), F32)
    for k in range(LEVEL):
        packed = held[k, 64:80]
        pt = jnp.concatenate([packed[:, 64 * j : 64 * (j + 1)] for j in range(4)], axis=0)
        total += dot(pt, held[k, 0:64], ((0,), (0,)))
    root = total.astype(BF)
    for z in range(Z):
        out_ref[z] = root


def after_kernel(*refs):
    pass


def ordered(arrays, after, name, **options):
    return pl.pallas_call(
        after_kernel,
        in_specs=[HBM] * (len(arrays) + len(after)),
        out_specs=[HBM] * len(arrays),
        out_shape=[jax.ShapeDtypeStruct(array.shape, array.dtype) for array in arrays],
        input_output_aliases={n: n for n in range(len(arrays))},
        compiler_params=params(60),
        name=name,
        **options,
    )(*arrays, *after)


def own_kernel(
    offset_ref, partner_ref, count_ref, u_hbm, nb_hbm, lb_hbm, bt_hbm, after_ref,
    acc_out, blocks_out, left_out, cross_out, slot_ref, far_slot, u, nb, lb, bt, own, blocks, left, acc,
    sem, out_sem, halo_sem,
):
    def load(src, dst, at):
        copy = pltpu.make_async_copy(src, dst, sem.at[at])
        copy.start()
        return copy

    small = [load(lb_hbm, lb, 0), load(bt_hbm, bt, 1)]
    tables = [load(nb_hbm.at[0], nb.at[0], 2)]
    units = load(u_hbm, u, 6)
    tables += [load(nb_hbm.at[i], nb.at[i], 2 + i) for i in range(1, 4)]
    for i in range(4):
        for o in range(9):
            slot_ref[i, o] = -1
            far_slot[i, o] = -1
        for s in range(8):
            slot_ref[i, offset_ref[i, s] + 4] = s
        for s in range(6):

            @pl.when(s < count_ref[i])
            def _():
                far_slot[i, partner_ref[i, s] + 4] = s

    for copy in small:
        copy.wait()
    zero = jnp.zeros((64, 64), BF)
    outward = []
    for g in range(4):
        cols = slice(256 * g, 256 * (g + 1))
        outward.append(pltpu.make_async_copy(bt.at[g], cross_out.at[1024:1088, cols], halo_sem.at[4 + g]))
        outward[-1].start()
    for i in range(4):
        rows = slice(256 * i, 256 * (i + 1))
        places = list(range(i, 4)) + list(range(8, i + 9)) + [w for w in OWN if w != i + 4]
        coupling = []
        for w in places:
            slot = far_slot[i, w - i]
            coupling.append(jnp.where(slot >= 0, lb[i, jnp.maximum(slot, 0)], zero))
        left_i = dot(bt[i].T, jnp.concatenate(coupling, axis=1)).astype(BF)
        left[rows] = left_i[:, 0:320]
        tables[i].wait()
        for k, w in enumerate(places):
            block = near_block(slot_ref, nb, i, w)
            if w in OWN:
                block = block.astype(F32) + dot(left_i[:, 64 * k : 64 * (k + 1)], bt[w - 4])
                own[:, 256 * (w - 4) : 256 * (w - 3)] = block.astype(BF)
            else:
                blocks[rows, 256 * k : 256 * (k + 1)] = block
        own[:, rows] = near_block(slot_ref, nb, i, i + 4)
        outward.append(pltpu.make_async_copy(blocks.at[rows], blocks_out.at[rows], out_sem.at[i]))
        outward[-1].start()
        if i == 0:
            units.wait()
            for g in range(4):
                outward.append(pltpu.make_async_copy(u.at[g], cross_out.at[256 * g : 256 * (g + 1)], halo_sem.at[g]))
                outward[-1].start()
        for half in range(2):
            cols = slice(512 * half, 512 * (half + 1))
            acc[i, :, cols] = dot(own[...], jnp.concatenate([u[w, :, cols] for w in range(4)], axis=0))
        outward.append(pltpu.make_async_copy(acc.at[i], acc_out.at[i], out_sem.at[4 + i]))
        outward[-1].start()
    outward.append(pltpu.make_async_copy(left, left_out, out_sem.at[8]))
    outward[-1].start()
    for copy in outward:
        copy.wait()


def folded(blocks, left, i, k, basis):
    rows = slice(256 * i, 256 * (i + 1))
    far = dot(left[rows, 64 * k : 64 * (k + 1)], basis)
    return (blocks[rows, 256 * k : 256 * (k + 1)].astype(F32) + far).astype(BF)


def top_kernel(source_ref, count_ref, own0, own1, own2, own3, other0, other1, other2, other3, msg_ref, after_ref, out_ref, table, blocks, sem, block_sem):
    copies = []
    for k, pair in enumerate(((own0, other0), (own1, other1), (own2, other2), (own3, other3))):
        for c in range(CORES):
            copies.append(pltpu.make_async_copy(pair[c], table.at[c, k], sem.at[c, k]))
    for k in range(LEVEL):
        copies.append(pltpu.make_async_copy(msg_ref.at[k, 80:208], blocks.at[k], block_sem.at[k]))
    for copy in copies:
        copy.start()
    for copy in copies:
        copy.wait()
    lead = lax.axis_index("leaf")
    my_x, my_core = lead // (Z * CORES), lax.rem(lead, CORES)
    total = jnp.zeros((64, 256), F32)
    for k in range(LEVEL):
        for half in range(2):
            rows = []
            for s in range(4):
                at = 8 * k + 4 * half + s
                source = source_ref[0, at]
                core = lax.rem(source + my_core, CORES)
                step = lax.rem(my_x - source // (Z * CORES) + X, X)
                row = table[core, step, lax.rem(source // CORES, Z)]
                rows.append(jnp.where(at < count_ref[0], row, jnp.zeros_like(row)))
            total += dot(blocks[k, 64 * half : 64 * (half + 1)], jnp.concatenate(rows, axis=0))
    for k in range(LEVEL):
        out_ref[k] = total.astype(BF)


def last_kernel(
    p_hbm, n_hbm, cross_hbm, blocks_hbm, left_hbm, acc_hbm, field_hbm, lt_hbm, pt_hbm, bt_hbm, out_ref,
    p, n, blocks, left, acc, field, lt, pt, bt, lines, leaves, held, sem, side_sem, out_sem,
):
    def load(src, dst, at):
        copy = pltpu.make_async_copy(src, dst, sem.at[at])
        copy.start()
        return copy

    lead, level = lax.axis_index("leaf"), lax.axis_index("level")
    core = lax.rem(lead, CORES)
    cross_prev = jnp.logical_and(level == 0, core == 0)
    cross_next = jnp.logical_and(level == LEVEL - 1, core == CORES - 1)
    pieces = ((slice(1024, 1088), slice(0, 1024)), (slice(0, 1024), slice(0, 512)), (slice(0, 1024), slice(512, 1024)))

    def side_copy(side, piece, src):
        rows, cols = pieces[piece]
        return pltpu.make_async_copy(src.at[rows, cols], (p, n)[side].at[rows, cols], side_sem.at[side, piece])

    def start_sides(wanted):
        for side, (inner, crossed) in enumerate(((p_hbm, cross_prev), (n_hbm, cross_next))):
            for src, here in ((inner, jnp.logical_not(crossed)), (cross_hbm, crossed)):

                @pl.when(here)
                def _():
                    for piece in wanted:
                        side_copy(side, piece, src).start()

    def wait_sides(piece):
        side_copy(0, piece, p_hbm).wait()
        side_copy(1, piece, n_hbm).wait()

    halves = (slice(0, 512), slice(512, 1024))
    targets = [slice(256 * i, 256 * (i + 1)) for i in range(4)]
    small = [load(left_hbm, left, 0), load(field_hbm, field, 1), load(lt_hbm, lt, 2), load(pt_hbm, pt, 3)]
    small.append(load(bt_hbm, bt, 4))
    tables = [load(blocks_hbm.at[targets[0]], blocks.at[targets[0]], 5)]
    start_sides((0, 1))
    sums = {}
    for half in range(2):
        for i in range(4):
            if half == 0 and i > 0:
                tables.append(load(blocks_hbm.at[targets[i]], blocks.at[targets[i]], 5 + i))
            sums[half, i] = load(acc_hbm.at[i, :, halves[half]], acc.at[i, :, halves[half]], 9 + 4 * half + i)
        if half == 0:
            start_sides((2,))

    for copy in small:
        copy.wait()
    parent = dot(pt[...], jnp.concatenate([field[q] for q in range(LEVEL)], axis=1))
    high = parent.astype(BF)
    low = (parent - high.astype(F32)).astype(BF)
    for i in range(4):
        transfer = lt[64 * i : 64 * (i + 1)]
        leaf = dot(transfer, high) + dot(transfer, low)
        leaf_high = leaf.astype(BF)
        leaves[i, 0:64] = leaf_high
        leaves[i, 64:128] = (leaf - leaf_high.astype(F32)).astype(BF)
    wait_sides(0)
    outward = []
    for half in range(2):
        cols = halves[half]
        for i in range(4):
            if half == 0:
                basis = bt[i].T
                tables[i].wait()
                for k in range(5):
                    ref, g = (p, i + k) if i + k < 4 else (n, i + k - 4)
                    part = folded(blocks, left, i, k, ref[1024:1088, 256 * g : 256 * (g + 1)])
                    lines[targets[i], 256 * k : 256 * (k + 1)] = part
                lines[targets[i], 1280:1408] = jnp.concatenate([basis, basis], axis=1)
            if i == 0:
                wait_sides(1 + half)
            sums[half, i].wait()
            sources = [p[256 * w : 256 * (w + 1), cols] for w in range(i, 4)]
            sources += [n[256 * w : 256 * (w + 1), cols] for w in range(i + 1)]
            sources.append(leaves[i, :, cols])
            held[i, :, cols] = acc[i, :, cols] + dot(lines[targets[i]], jnp.concatenate(sources, axis=0))
            copy = pltpu.make_async_copy(held.at[i, :, cols], out_ref.at[i, :, cols], out_sem.at[half, i])
            copy.start()
            outward.append(copy)
    for copy in outward:
        copy.wait()


def params(mib):
    return pltpu.CompilerParams(vmem_limit_bytes=mib * MIB)


VMEM = pl.BlockSpec(memory_space=pltpu.VMEM)
SMEM = pl.BlockSpec(memory_space=pltpu.SMEM)
ANY = pl.BlockSpec(memory_space=pl.ANY)
HBM = pl.BlockSpec(memory_space=pltpu.HBM)


def body(
    unknowns, leaf_basis, leaf_transfer, parent_transfer, near_blocks, near_offset,
    leaf_blocks, leaf_partner, leaf_count, top_blocks, top_source, top_count,
):
    both = ("leaf", "level")
    total = lax.axis_size("leaf") * LEVEL
    ahead = [(i, i + 1) for i in range(total - 1)]
    back = [(i + 1, i) for i in range(total - 1)]

    def crossing(a):
        return a % LEVEL == LEVEL - 1 and a // LEVEL % CORES == CORES - 1

    bt = leaf_basis.transpose(0, 2, 1)
    lt = leaf_transfer.reshape(256, 64)
    pt = parent_transfer[0]

    pieces, message = pl.pallas_call(
        moments_kernel,
        in_specs=[HBM] * 5,
        out_specs=[VMEM, HBM],
        out_shape=[jax.ShapeDtypeStruct((LEVEL, 208, 256), BF)] + [jax.ShapeDtypeStruct((1088, 1024), BF)],
        scratch_shapes=[
            pltpu.VMEM((256, 1024), BF), pltpu.VMEM((4, 256, 1024), BF), pltpu.VMEM((4, 64, 256), BF),
            pltpu.VMEM((256, 64), BF), pltpu.VMEM((64, 64), BF), pltpu.VMEM((8, 64, 64), BF),
            pltpu.SemaphoreType.DMA((8,)), pltpu.SemaphoreType.DMA((1, 8)),
        ],
        compiler_params=params(60),
        name="moments",
    )(unknowns, bt, lt, pt, top_blocks[0])

    heap = lax.all_to_all(pieces, "level", 0, 0, tiled=True)

    (message,) = ordered([message], [heap], "send_inner")
    inner = lambda pairs: [(a, b) for a, b in pairs if not crossing(min(a, b))]
    inner_prev = lax.ppermute(message, both, inner(ahead))
    inner_next = lax.ppermute(message, both, inner(back))

    root = pl.pallas_call(
        roots_kernel,
        in_specs=[HBM] * 2,
        out_specs=VMEM,
        out_shape=jax.ShapeDtypeStruct((Z, 64, 256), BF),
        scratch_shapes=[pltpu.VMEM((LEVEL, 80, 256), BF), pltpu.SemaphoreType.DMA],
        compiler_params=params(60),
        name="roots",
    )(heap, message)

    def place(x, z, c):
        return (x * Z + z) * CORES + c

    leaves = [(x, z, c) for x in range(X) for z in range(Z) for c in range(CORES)]
    along_x = lambda step: [(place(x, z, c), place((x + step) % X, z, c)) for x, z, c in leaves]
    swap = [(place(x, z, c), place(x, z, 1 - c)) for x, z, c in leaves]
    groups = [[place(x, z, c) for z in range(Z)] for x in range(X) for c in range(CORES)]
    column = lax.all_to_all(root, "leaf", 0, 0, axis_index_groups=groups, tiled=True)
    acc_shape = jax.ShapeDtypeStruct((4, 256, 1024), F32)
    acc, blocks, left, cross_message = pl.pallas_call(
        own_kernel,
        in_specs=[SMEM] * 3 + [HBM] * 5,
        out_specs=[HBM] * 4,
        out_shape=[
            acc_shape, jax.ShapeDtypeStruct((1024, 1280), BF), jax.ShapeDtypeStruct((1024, 320), BF),
            jax.ShapeDtypeStruct((1088, 1024), BF),
        ],
        scratch_shapes=[
            pltpu.SMEM((4, 9), jnp.int32), pltpu.SMEM((4, 9), jnp.int32), pltpu.VMEM((4, 256, 1024), BF),
            pltpu.VMEM((4, 8, 256, 256), BF), pltpu.VMEM((4, 6, 64, 64), BF), pltpu.VMEM((4, 64, 256), BF),
            pltpu.VMEM((256, 1024), BF), pltpu.VMEM((1024, 1280), BF), pltpu.VMEM((1024, 320), BF),
            pltpu.VMEM((4, 256, 1024), F32), pltpu.SemaphoreType.DMA((7,)), pltpu.SemaphoreType.DMA((9,)),
            pltpu.SemaphoreType.DMA((8,)),
        ],
        compiler_params=params(60),
        cost_estimate=pl.CostEstimate(flops=6_000_000_000, bytes_accessed=16 * MIB, transcendentals=0),
        name="near_own",
    )(near_offset, leaf_partner, leaf_count, unknowns, near_blocks, leaf_blocks, bt, column)

    mine = [lax.ppermute(column, "leaf", along_x(step)) for step in range(1, X)]
    mine = [column] + list(ordered(mine, [left], "gathered"))
    theirs = [lax.ppermute(m, "leaf", swap) for m in mine]
    (cross_message,) = ordered([cross_message], [mine[1]], "send_crossing")
    cross = lax.ppermute(cross_message, both, [(a, b) for a, b in ahead + back if crossing(min(a, b))])

    field = pl.pallas_call(
        top_kernel,
        in_specs=[SMEM, SMEM] + [HBM] * 10,
        out_specs=VMEM,
        scratch_shapes=[
            pltpu.VMEM((CORES, X, Z, 64, 256), BF), pltpu.VMEM((LEVEL, 128, 256), BF),
            pltpu.SemaphoreType.DMA((CORES, X)), pltpu.SemaphoreType.DMA((LEVEL,)),
        ],
        out_shape=jax.ShapeDtypeStruct((LEVEL, 64, 256), BF),
        compiler_params=params(60),
        name="top",
    )(top_source, top_count, *mine, *theirs, heap, left)
    fields = lax.all_to_all(field, "level", 0, 0, tiled=True)

    inner_prev, inner_next = ordered(
        [inner_prev, inner_next], [left], "arrived",
        cost_estimate=pl.CostEstimate(flops=8_000_000_000, bytes_accessed=16 * MIB, transcendentals=0),
    )
    return pl.pallas_call(
        last_kernel,
        in_specs=[HBM] * 10,
        out_specs=HBM,
        out_shape=acc_shape,
        scratch_shapes=[
            pltpu.VMEM((1088, 1024), BF), pltpu.VMEM((1088, 1024), BF), pltpu.VMEM((1024, 1280), BF),
            pltpu.VMEM((1024, 320), BF), pltpu.VMEM((4, 256, 1024), F32), pltpu.VMEM((LEVEL, 64, 256), BF),
            pltpu.VMEM((256, 64), BF), pltpu.VMEM((64, 64), BF), pltpu.VMEM((4, 64, 256), BF),
            pltpu.VMEM((1024, 1408), BF), pltpu.VMEM((4, 128, 1024), BF), pltpu.VMEM((4, 256, 1024), F32),
            pltpu.SemaphoreType.DMA((17,)), pltpu.SemaphoreType.DMA((2, 3)), pltpu.SemaphoreType.DMA((2, 4)),
        ],
        compiler_params=params(60),
        name="product",
    )(inner_prev, inner_next, cross, blocks, left, acc, fields, lt, pt, bt)


def solution(mesh):
    return jax.shard_map(
        body,
        mesh=mesh,
        in_specs=(
            P(("leaf", "level"), None, None),
            P(("leaf", "level"), None, None),
            P(("leaf", "level"), None, None),
            P(("leaf", "level"), None, None),
            P(("leaf", "level"), None, None, None),
            P(("leaf", "level"), None),
            P(("leaf", "level"), None, None, None),
            P(("leaf", "level"), None),
            P(("leaf", "level")),
            P("leaf", "level", None, None),
            P("leaf", None),
            P("leaf"),
        ),
        out_specs=P(("leaf", "level"), None, None),
        check_vma=False,
    )
```

```python
import functools

import jax
import jax.numpy as jnp
from jax import lax
from jax.experimental import pallas as pl
from jax.experimental.pallas import tpu as pltpu
from jax.sharding import PartitionSpec as P

X, Z, CORES = 4, 8, 2
LEVEL = 4
BF = jnp.bfloat16
F32 = jnp.float32
MIB = 1 << 20

OWN = (4, 5, 6, 7)
HALO = (0, 1, 2, 3, 8, 9, 10, 11)


def dot(a, b, dims=((1,), (0,))):
    return lax.dot_general(a, b, (dims, ((), ())), preferred_element_type=F32)


def near_block(slot_ref, nb_ref, target, place):
    slot = slot_ref[target, place - target]
    block = nb_ref[target, jnp.maximum(slot, 0)]
    return jnp.where(slot >= 0, block, jnp.zeros_like(block))


def moments_kernel(
    u_ref, bt_ref, lt_ref, pt_ref, tb_ref, msg_ref, out_ref, m_ref, u, bt, lt, pt, tb, sem, out_sem
):
    small = [
        pltpu.make_async_copy(src, dst, sem.at[4 + n])
        for n, (src, dst) in enumerate(((bt_ref, bt), (lt_ref, lt), (pt_ref, pt), (tb_ref, tb)))
    ]
    large = [pltpu.make_async_copy(u_ref.at[g], u.at[g], sem.at[g]) for g in range(4)]
    units, bases = [], []
    for n, ref in enumerate((out_ref,)):
        for g in range(4):
            rows = slice(256 * g, 256 * (g + 1))
            units.append(pltpu.make_async_copy(u.at[g], ref.at[rows], out_sem.at[n, g]))
            bases.append(pltpu.make_async_copy(bt.at[g], ref.at[1024:1088, rows], out_sem.at[n, 4 + g]))
    small[0].start()
    for copy in large + small[1:]:
        copy.start()
    small[0].wait()
    for copy in bases:
        copy.start()
    for g in range(4):
        large[g].wait()
        units[g].start()
        m_ref[64 * g : 64 * (g + 1)] = dot(bt[g], u[g]).astype(BF)
    for copy in small[1:]:
        copy.wait()
    parent = dot(lt[...], m_ref[...], ((0,), (0,))).astype(BF)
    packed = jnp.concatenate([pt[16 * j : 16 * (j + 1)] for j in range(4)], axis=1)
    blocks = [jnp.concatenate([tb[4 * half + s] for s in range(4)], axis=1) for half in range(2)]
    for q in range(LEVEL):
        msg_ref[q, 0:64] = parent[:, 256 * q : 256 * (q + 1)]
        msg_ref[q, 64:80] = packed
        msg_ref[q, 80:144] = blocks[0]
        msg_ref[q, 144:208] = blocks[1]
    for copy in units + bases:
        copy.wait()


def roots_kernel(msg_ref, after_ref, out_ref, held, sem):
    copy = pltpu.make_async_copy(msg_ref.at[:, 0:80], held, sem)
    copy.start()
    copy.wait()
    total = jnp.zeros((64, 256), F32)
    for k in range(LEVEL):
        packed = held[k, 64:80]
        pt = jnp.concatenate([packed[:, 64 * j : 64 * (j + 1)] for j in range(4)], axis=0)
        total += dot(pt, held[k, 0:64], ((0,), (0,)))
    root = total.astype(BF)
    for z in range(Z):
        out_ref[z] = root


def after_kernel(*refs):
    pass


def ordered(arrays, after, name, **options):
    return pl.pallas_call(
        after_kernel,
        in_specs=[HBM] * (len(arrays) + len(after)),
        out_specs=[HBM] * len(arrays),
        out_shape=[jax.ShapeDtypeStruct(array.shape, array.dtype) for array in arrays],
        input_output_aliases={n: n for n in range(len(arrays))},
        compiler_params=params(60),
        name=name,
        **options,
    )(*arrays, *after)


def own_kernel(
    offset_ref, partner_ref, count_ref, u_hbm, nb_hbm, lb_hbm, bt_hbm, after_ref,
    acc_out, blocks_out, left_out, cross_out, slot_ref, far_slot, u, nb, lb, bt, own, blocks, left, acc,
    sem, out_sem, halo_sem,
):
    def load(src, dst, at):
        copy = pltpu.make_async_copy(src, dst, sem.at[at])
        copy.start()
        return copy

    small = [load(lb_hbm, lb, 0), load(bt_hbm, bt, 1)]
    tables = [load(nb_hbm.at[0], nb.at[0], 2)]
    units = load(u_hbm, u, 6)
    tables += [load(nb_hbm.at[i], nb.at[i], 2 + i) for i in range(1, 4)]
    for i in range(4):
        for o in range(9):
            slot_ref[i, o] = -1
            far_slot[i, o] = -1
        for s in range(8):
            slot_ref[i, offset_ref[i, s] + 4] = s
        for s in range(6):

            @pl.when(s < count_ref[i])
            def _():
                far_slot[i, partner_ref[i, s] + 4] = s

    for copy in small:
        copy.wait()
    zero = jnp.zeros((64, 64), BF)
    outward = []
    for g in range(4):
        cols = slice(256 * g, 256 * (g + 1))
        outward.append(pltpu.make_async_copy(bt.at[g], cross_out.at[1024:1088, cols], halo_sem.at[4 + g]))
        outward[-1].start()
    for i in range(4):
        rows = slice(256 * i, 256 * (i + 1))
        places = list(range(i, 4)) + list(range(8, i + 9)) + [w for w in OWN if w != i + 4]
        coupling = []
        for w in places:
            slot = far_slot[i, w - i]
            coupling.append(jnp.where(slot >= 0, lb[i, jnp.maximum(slot, 0)], zero))
        left_i = dot(bt[i].T, jnp.concatenate(coupling, axis=1)).astype(BF)
        left[rows] = left_i[:, 0:320]
        tables[i].wait()
        for k, w in enumerate(places):
            block = near_block(slot_ref, nb, i, w)
            if w in OWN:
                block = block.astype(F32) + dot(left_i[:, 64 * k : 64 * (k + 1)], bt[w - 4])
                own[:, 256 * (w - 4) : 256 * (w - 3)] = block.astype(BF)
            else:
                blocks[rows, 256 * k : 256 * (k + 1)] = block
        own[:, rows] = near_block(slot_ref, nb, i, i + 4)
        outward.append(pltpu.make_async_copy(blocks.at[rows], blocks_out.at[rows], out_sem.at[i]))
        outward[-1].start()
        if i == 0:
            units.wait()
            for g in range(4):
                outward.append(pltpu.make_async_copy(u.at[g], cross_out.at[256 * g : 256 * (g + 1)], halo_sem.at[g]))
                outward[-1].start()
        for half in range(2):
            cols = slice(512 * half, 512 * (half + 1))
            acc[i, :, cols] = dot(own[...], jnp.concatenate([u[w, :, cols] for w in range(4)], axis=0)).astype(BF)
        outward.append(pltpu.make_async_copy(acc.at[i], acc_out.at[i], out_sem.at[4 + i]))
        outward[-1].start()
    outward.append(pltpu.make_async_copy(left, left_out, out_sem.at[8]))
    outward[-1].start()
    for copy in outward:
        copy.wait()


def folded(blocks, left, i, k, basis):
    rows = slice(256 * i, 256 * (i + 1))
    far = dot(left[rows, 64 * k : 64 * (k + 1)], basis)
    return (blocks[rows, 256 * k : 256 * (k + 1)].astype(F32) + far).astype(BF)


def top_kernel(source_ref, count_ref, own0, own1, own2, own3, other0, other1, other2, other3, msg_ref, after_ref, out_ref, table, blocks, sem, block_sem):
    copies = []
    for k, pair in enumerate(((own0, other0), (own1, other1), (own2, other2), (own3, other3))):
        for c in range(CORES):
            copies.append(pltpu.make_async_copy(pair[c], table.at[c, k], sem.at[c, k]))
    for k in range(LEVEL):
        copies.append(pltpu.make_async_copy(msg_ref.at[k, 80:208], blocks.at[k], block_sem.at[k]))
    for copy in copies:
        copy.start()
    for copy in copies:
        copy.wait()
    lead = lax.axis_index("leaf")
    my_x, my_core = lead // (Z * CORES), lax.rem(lead, CORES)
    total = jnp.zeros((64, 256), F32)
    for k in range(LEVEL):
        for half in range(2):
            rows = []
            for s in range(4):
                at = 8 * k + 4 * half + s
                source = source_ref[0, at]
                core = lax.rem(source + my_core, CORES)
                step = lax.rem(my_x - source // (Z * CORES) + X, X)
                row = table[core, step, lax.rem(source // CORES, Z)]
                rows.append(jnp.where(at < count_ref[0], row, jnp.zeros_like(row)))
            total += dot(blocks[k, 64 * half : 64 * (half + 1)], jnp.concatenate(rows, axis=0))
    for k in range(LEVEL):
        out_ref[k] = total.astype(BF)


def last_kernel(
    p_hbm, n_hbm, cross_hbm, blocks_hbm, left_hbm, acc_hbm, field_hbm, lt_hbm, pt_hbm, bt_hbm, out_ref,
    p, n, blocks, left, acc, field, lt, pt, bt, lines, leaves, held, sem, side_sem, out_sem,
):
    def load(src, dst, at):
        copy = pltpu.make_async_copy(src, dst, sem.at[at])
        copy.start()
        return copy

    lead, level = lax.axis_index("leaf"), lax.axis_index("level")
    core = lax.rem(lead, CORES)
    cross_prev = jnp.logical_and(level == 0, core == 0)
    cross_next = jnp.logical_and(level == LEVEL - 1, core == CORES - 1)
    pieces = ((slice(1024, 1088), slice(0, 1024)), (slice(0, 1024), slice(0, 512)), (slice(0, 1024), slice(512, 1024)))

    def side_copy(side, piece, src):
        rows, cols = pieces[piece]
        return pltpu.make_async_copy(src.at[rows, cols], (p, n)[side].at[rows, cols], side_sem.at[side, piece])

    def start_sides(wanted):
        for side, (inner, crossed) in enumerate(((p_hbm, cross_prev), (n_hbm, cross_next))):
            for src, here in ((inner, jnp.logical_not(crossed)), (cross_hbm, crossed)):

                @pl.when(here)
                def _():
                    for piece in wanted:
                        side_copy(side, piece, src).start()

    def wait_sides(piece):
        side_copy(0, piece, p_hbm).wait()
        side_copy(1, piece, n_hbm).wait()

    halves = (slice(0, 512), slice(512, 1024))
    targets = [slice(256 * i, 256 * (i + 1)) for i in range(4)]
    small = [load(left_hbm, left, 0), load(field_hbm, field, 1), load(lt_hbm, lt, 2), load(pt_hbm, pt, 3)]
    small.append(load(bt_hbm, bt, 4))
    tables = [load(blocks_hbm.at[targets[0]], blocks.at[targets[0]], 5)]
    start_sides((0, 1))
    sums = {}
    for half in range(2):
        for i in range(4):
            if half == 0 and i > 0:
                tables.append(load(blocks_hbm.at[targets[i]], blocks.at[targets[i]], 5 + i))
            sums[half, i] = load(acc_hbm.at[i, :, halves[half]], acc.at[i, :, halves[half]], 9 + 4 * half + i)
        if half == 0:
            start_sides((2,))

    for copy in small:
        copy.wait()
    parent = dot(pt[...], jnp.concatenate([field[q] for q in range(LEVEL)], axis=1))
    high = parent.astype(BF)
    low = (parent - high.astype(F32)).astype(BF)
    for i in range(4):
        transfer = lt[64 * i : 64 * (i + 1)]
        leaf = dot(transfer, high) + dot(transfer, low)
        leaf_high = leaf.astype(BF)
        leaves[i, 0:64] = leaf_high
        leaves[i, 64:128] = (leaf - leaf_high.astype(F32)).astype(BF)
    wait_sides(0)
    outward = []
    for half in range(2):
        cols = halves[half]
        for i in range(4):
            if half == 0:
                basis = bt[i].T
                tables[i].wait()
                for k in range(5):
                    ref, g = (p, i + k) if i + k < 4 else (n, i + k - 4)
                    part = folded(blocks, left, i, k, ref[1024:1088, 256 * g : 256 * (g + 1)])
                    lines[targets[i], 256 * k : 256 * (k + 1)] = part
                lines[targets[i], 1280:1408] = jnp.concatenate([basis, basis], axis=1)
            if i == 0:
                wait_sides(1 + half)
            sums[half, i].wait()
            sources = [p[256 * w : 256 * (w + 1), cols] for w in range(i, 4)]
            sources += [n[256 * w : 256 * (w + 1), cols] for w in range(i + 1)]
            sources.append(leaves[i, :, cols])
            held[i, :, cols] = acc[i, :, cols].astype(F32) + dot(lines[targets[i]], jnp.concatenate(sources, axis=0))
            copy = pltpu.make_async_copy(held.at[i, :, cols], out_ref.at[i, :, cols], out_sem.at[half, i])
            copy.start()
            outward.append(copy)
    for copy in outward:
        copy.wait()


def params(mib):
    return pltpu.CompilerParams(vmem_limit_bytes=mib * MIB)


VMEM = pl.BlockSpec(memory_space=pltpu.VMEM)
SMEM = pl.BlockSpec(memory_space=pltpu.SMEM)
ANY = pl.BlockSpec(memory_space=pl.ANY)
HBM = pl.BlockSpec(memory_space=pltpu.HBM)


def body(
    unknowns, leaf_basis, leaf_transfer, parent_transfer, near_blocks, near_offset,
    leaf_blocks, leaf_partner, leaf_count, top_blocks, top_source, top_count,
):
    both = ("leaf", "level")
    total = lax.axis_size("leaf") * LEVEL
    ahead = [(i, i + 1) for i in range(total - 1)]
    back = [(i + 1, i) for i in range(total - 1)]

    def crossing(a):
        return a % LEVEL == LEVEL - 1 and a // LEVEL % CORES == CORES - 1

    bt = leaf_basis.transpose(0, 2, 1)
    lt = leaf_transfer.reshape(256, 64)
    pt = parent_transfer[0]

    pieces, message = pl.pallas_call(
        moments_kernel,
        in_specs=[HBM] * 5,
        out_specs=[VMEM, HBM],
        out_shape=[jax.ShapeDtypeStruct((LEVEL, 208, 256), BF)] + [jax.ShapeDtypeStruct((1088, 1024), BF)],
        scratch_shapes=[
            pltpu.VMEM((256, 1024), BF), pltpu.VMEM((4, 256, 1024), BF), pltpu.VMEM((4, 64, 256), BF),
            pltpu.VMEM((256, 64), BF), pltpu.VMEM((64, 64), BF), pltpu.VMEM((8, 64, 64), BF),
            pltpu.SemaphoreType.DMA((8,)), pltpu.SemaphoreType.DMA((1, 8)),
        ],
        compiler_params=params(60),
        name="moments",
    )(unknowns, bt, lt, pt, top_blocks[0])

    heap = lax.all_to_all(pieces, "level", 0, 0, tiled=True)

    (message,) = ordered([message], [heap], "send_inner")
    inner = lambda pairs: [(a, b) for a, b in pairs if not crossing(min(a, b))]
    inner_prev = lax.ppermute(message, both, inner(ahead))
    inner_next = lax.ppermute(message, both, inner(back))

    root = pl.pallas_call(
        roots_kernel,
        in_specs=[HBM] * 2,
        out_specs=VMEM,
        out_shape=jax.ShapeDtypeStruct((Z, 64, 256), BF),
        scratch_shapes=[pltpu.VMEM((LEVEL, 80, 256), BF), pltpu.SemaphoreType.DMA],
        compiler_params=params(60),
        name="roots",
    )(heap, message)

    def place(x, z, c):
        return (x * Z + z) * CORES + c

    leaves = [(x, z, c) for x in range(X) for z in range(Z) for c in range(CORES)]
    along_x = lambda step: [(place(x, z, c), place((x + step) % X, z, c)) for x, z, c in leaves]
    swap = [(place(x, z, c), place(x, z, 1 - c)) for x, z, c in leaves]
    groups = [[place(x, z, c) for z in range(Z)] for x in range(X) for c in range(CORES)]
    column = lax.all_to_all(root, "leaf", 0, 0, axis_index_groups=groups, tiled=True)
    acc_shape = jax.ShapeDtypeStruct((4, 256, 1024), F32)
    acc, blocks, left, cross_message = pl.pallas_call(
        own_kernel,
        in_specs=[SMEM] * 3 + [HBM] * 5,
        out_specs=[HBM] * 4,
        out_shape=[
            jax.ShapeDtypeStruct((4, 256, 1024), BF), jax.ShapeDtypeStruct((1024, 1280), BF), jax.ShapeDtypeStruct((1024, 320), BF),
            jax.ShapeDtypeStruct((1088, 1024), BF),
        ],
        scratch_shapes=[
            pltpu.SMEM((4, 9), jnp.int32), pltpu.SMEM((4, 9), jnp.int32), pltpu.VMEM((4, 256, 1024), BF),
            pltpu.VMEM((4, 8, 256, 256), BF), pltpu.VMEM((4, 6, 64, 64), BF), pltpu.VMEM((4, 64, 256), BF),
            pltpu.VMEM((256, 1024), BF), pltpu.VMEM((1024, 1280), BF), pltpu.VMEM((1024, 320), BF),
            pltpu.VMEM((4, 256, 1024), BF), pltpu.SemaphoreType.DMA((7,)), pltpu.SemaphoreType.DMA((9,)),
            pltpu.SemaphoreType.DMA((8,)),
        ],
        compiler_params=params(60),
        cost_estimate=pl.CostEstimate(flops=6_000_000_000, bytes_accessed=16 * MIB, transcendentals=0),
        name="near_own",
    )(near_offset, leaf_partner, leaf_count, unknowns, near_blocks, leaf_blocks, bt, column)

    mine = [lax.ppermute(column, "leaf", along_x(step)) for step in range(1, X)]
    mine = [column] + list(ordered(mine, [left], "gathered"))
    theirs = [lax.ppermute(m, "leaf", swap) for m in mine]
    (cross_message,) = ordered([cross_message], [mine[1]], "send_crossing")
    cross = lax.ppermute(cross_message, both, [(a, b) for a, b in ahead + back if crossing(min(a, b))])

    field = pl.pallas_call(
        top_kernel,
        in_specs=[SMEM, SMEM] + [HBM] * 10,
        out_specs=VMEM,
        scratch_shapes=[
            pltpu.VMEM((CORES, X, Z, 64, 256), BF), pltpu.VMEM((LEVEL, 128, 256), BF),
            pltpu.SemaphoreType.DMA((CORES, X)), pltpu.SemaphoreType.DMA((LEVEL,)),
        ],
        out_shape=jax.ShapeDtypeStruct((LEVEL, 64, 256), BF),
        compiler_params=params(60),
        name="top",
    )(top_source, top_count, *mine, *theirs, heap, left)
    fields = lax.all_to_all(field, "level", 0, 0, tiled=True)

    inner_prev, inner_next = ordered(
        [inner_prev, inner_next], [left], "arrived",
        cost_estimate=pl.CostEstimate(flops=8_000_000_000, bytes_accessed=16 * MIB, transcendentals=0),
    )
    return pl.pallas_call(
        last_kernel,
        in_specs=[HBM] * 10,
        out_specs=HBM,
        out_shape=acc_shape,
        scratch_shapes=[
            pltpu.VMEM((1088, 1024), BF), pltpu.VMEM((1088, 1024), BF), pltpu.VMEM((1024, 1280), BF),
            pltpu.VMEM((1024, 320), BF), pltpu.VMEM((4, 256, 1024), BF), pltpu.VMEM((LEVEL, 64, 256), BF),
            pltpu.VMEM((256, 64), BF), pltpu.VMEM((64, 64), BF), pltpu.VMEM((4, 64, 256), BF),
            pltpu.VMEM((1024, 1408), BF), pltpu.VMEM((4, 128, 1024), BF), pltpu.VMEM((4, 256, 1024), F32),
            pltpu.SemaphoreType.DMA((17,)), pltpu.SemaphoreType.DMA((2, 3)), pltpu.SemaphoreType.DMA((2, 4)),
        ],
        compiler_params=params(60),
        name="product",
    )(inner_prev, inner_next, cross, blocks, left, acc, fields, lt, pt, bt)


def solution(mesh):
    return jax.shard_map(
        body,
        mesh=mesh,
        in_specs=(
            P(("leaf", "level"), None, None),
            P(("leaf", "level"), None, None),
            P(("leaf", "level"), None, None),
            P(("leaf", "level"), None, None),
            P(("leaf", "level"), None, None, None),
            P(("leaf", "level"), None),
            P(("leaf", "level"), None, None, None),
            P(("leaf", "level"), None),
            P(("leaf", "level")),
            P("leaf", "level", None, None),
            P("leaf", None),
            P("leaf"),
        ),
        out_specs=P(("leaf", "level"), None, None),
        check_vma=False,
    )
```
